32 devices in a mesh: parts: 2 (over x), tile: 16 (over z, y, core).
Axes of the slice: x: 2, y: 2, z: 4, core: 2. Of those that a mesh axis runs over, the one named last changes fastest.
Arguments:
- tiles: bfloat16 [64, 16, 16, 256], P(('parts', 'tile')), parts along dimension 0, may hold values from -6 to 6
- source_device: int32 [64, 8, 1], P(('parts', 'tile')), parts along dimension 0, may hold values from 0 to 15; in each aligned block of 16 rows (0 to 15, 16 to 31, ..., all dimensions but the last counted through in order) at most 2 rows name the same one
- source_slot: int32 [64, 8], P(('parts', 'tile')), parts along dimension 0, may hold values from 0 to 1
- present: int32 [64, 8], P(('parts', 'tile')), parts along dimension 0, may hold values 0 or 1
- depth_kernel: float32 [2, 49, 256], replicated, may hold values from -10 to 10
- norm_gain: float32 [2, 256], replicated, may hold values from 0.1 to 1.9
- w_in: bfloat16 [2, 256, 1024], replicated, may hold values from -0.375 to 0.375
- w_out: bfloat16 [2, 1024, 256], replicated, may hold values from -0.1875 to 0.1875
- cotangent: bfloat16 [64, 16, 16, 256], P(('parts', 'tile')), parts along dimension 0, may hold values from -6 to 6
Outputs:
- grad_tiles: bfloat16 [64, 16, 16, 256], P(('parts', 'tile')), parts along dimension 0
- grad_in: float32 [512, 2, 1024], P(('parts', 'tile')), parts along dimension 0
- grad_out: float32 [512, 2, 1024], P(('parts', 'tile')), parts along dimension 0
- grad_kernel: float32 [4, 49, 256], P('parts'), parts along dimension 0
- grad_gain: float32 [4, 256], P('parts'), parts along dimension 0
The draws below stay inside these ranges and needn't reach their ends.
There are 2 independent parts, one for each index of `parts`. The reference program is written for one: setup_inputs(seed, part) draws one part's arguments, and reference() takes and returns one part's arrays. A program takes and returns all parts, laid end to end along the dimension named above; an argument that names none is the same for every part. Nothing has to cross between parts.
Inputs may be any that keep to these rules, and one draw needn't show every extreme that they name: `source_device`: among the 16 rows of one device (its tiles times the 8 directions) no device index appears more than 2 times, and 2 is reached.
All inputs are finite; a program needn't handle non-finite values. No bound on the sum of `present` on one device may be relied on, other than what follows from the above.
Results may differ from the reference program's by a relative error of at most 0.007.
Values may be sent and summed in bfloat16 or wider, within the bound.
A program may use at most 128 MiB of HBM per device.

```python
import math
import jax
import jax.numpy as jnp
import numpy as np
from jax import lax

C = 256
H = 1024
NB = 2
TP = 16
TILES_DEV = 2
TILES = 32
MOST = 2
PIXELS = 8192
N_TILE = 16


def draw_depth_kernel(key, part):
    first_key, second_key = jax.random.split(key, 2)
    scales = jnp.exp(jax.random.uniform(first_key, (NB, 1, C), jnp.float32, 0.0, math.log(10.0)))
    taps = jnp.clip(jax.random.normal(second_key, (NB, 49, C), jnp.float32), -4.0, 4.0)
    return taps * scales / 7.0


def set_ends(values, own_key, low, largest):
    dims = values.shape
    place = [jax.random.randint(jax.random.fold_in(own_key, axis), (), 0, dims[axis]) for axis in range(len(dims))]
    values = values.at[tuple(place)].set(low)
    longest = dims.index(max(dims))
    place[longest] = (place[longest] + 1) % dims[longest]
    return values.at[tuple(place)].set(largest)


def strengthened(result, rng, source, target, blocks, factor):
    def block_of(dim):
        return (jnp.arange(result.shape[dim]) // (result.shape[dim] // blocks)).reshape((-1,) + (1,) * (result.ndim - 1 - dim))

    near = jax.random.permutation(rng, blocks)[block_of(target)]
    second = (block_of(target) + blocks // 2) % blocks
    return jnp.where((block_of(source) == near) | (block_of(source) == second), factor * result, result)


def shard_levels(key, dims, shards, smallest, top_value):
    factor_of, own = 1.0, jax.random.fold_in(key, 6)
    for dim, blocks in shards:
        heights = jnp.exp(jax.random.uniform(jax.random.fold_in(own, dim), (blocks,), jnp.float32, smallest / len(shards), top_value / len(shards)))
        factor_of = factor_of * jnp.repeat(heights, dims[dim] // blocks).reshape([-1 if axis == dim else 1 for axis in range(len(dims))])
    return factor_of


def deal_out(key, own, number, rows, count, top, bound, lean):
    order = jax.random.permutation(key, count)
    packed, common = load_shares(count, rows * top, bound, lean, True), load_shares(count, rows * top, bound, lean, False)
    places = jnp.arange(count)

    def named(lengths, rotation):
        used = int((lengths > 0).sum())
        fixed = max(1, used // 4)
        moved = fixed + (places - fixed + rotation * (used - fixed)) % max(1, count - fixed)
        return jnp.zeros((count,), jnp.int32).at[order[jnp.where(places < fixed, places, moved)]].set(jnp.asarray(lengths, jnp.int32))

    lengths = jnp.where(number % 4 == 0, named(packed, number // 4), named(common, number - number // 4 - 1))
    mixed = jax.random.permutation(jax.random.fold_in(own, 3), count)
    giver, sink = mixed[0:count // 2 * 2:2], mixed[1:count // 2 * 2:2]
    slack = jnp.minimum(lengths[giver] - 1, bound - lengths[sink]) // 2
    slack = jnp.where((giver == order[0]) | (sink == order[0]) | (lengths[sink] == 0), 0, jnp.maximum(slack, 0))
    moved = jax.random.randint(jax.random.fold_in(own, 4), (count // 2,), 0, 1 << 20) % (slack + 1)
    lengths = lengths.at[giver].add(-moved).at[sink].add(moved)
    labels = jnp.searchsorted(jnp.cumsum(lengths), jnp.arange(rows * top), side="right").astype(jnp.int32)
    table = labels.reshape(top, rows).T
    table = table[jax.random.permutation(jax.random.fold_in(own, 1), rows)]
    rotation = jax.random.randint(jax.random.fold_in(own, 2), (rows, 1), 0, top)
    return jnp.take_along_axis(table, (jnp.arange(top)[None, :] + rotation) % top, axis=1)


def load_shares(amount, total, most, skew, full):
    loads = [(1 << 20) // math.isqrt(grade ** skew) + 1 for grade in range(1, amount + 1)]
    largest = most if full else min(most, max(-(-total // amount), total * loads[0] // sum(loads)))
    least = 1 if total - largest >= amount - 1 else 0
    counts, rest = [largest] + [least] * (amount - 1), total - largest - least * (amount - 1)
    while rest > 0:
        movable = [i for i in range(1, amount) if counts[i] < largest] or [i for i in range(1, amount) if counts[i] < most]
        mass, remaining = sum([loads[i] for i in movable]), rest
        for i in movable:
            addition = min(most - counts[i], max(1, remaining * loads[i] // mass), rest)
            counts[i] = counts[i] + addition
            rest = rest - addition
    return np.array(counts)


def noise(rng, shape, width, reach, cuts=(), kind=jnp.bfloat16):
    level = shard_levels(rng, shape, cuts, -0.22, 0.18) if cuts else 1.0
    entries = jax.random.normal(rng, shape, jnp.float32) * width * level
    return jnp.minimum(jnp.maximum(entries, -reach), reach).astype(kind)


def gaussian_with(rng, shape, scale, reach, cuts, heavy, kind=jnp.bfloat16):
    result = scale * jax.random.normal(rng, shape, jnp.float32)
    if cuts:
        result = result * shard_levels(rng, shape, cuts, -0.22, 0.18)
    return jnp.clip(strengthened(result, jax.random.fold_in(rng, 3), *heavy), -reach, reach).astype(kind)


def setup_inputs(seed: int = 0, part: int = 0) -> dict:
    key_list = jax.random.split(jax.random.key(seed), 10)
    part_splits = jax.random.split(jax.random.fold_in(key_list[9], part), 10)
    tiles = noise(part_splits[0], (TILES, TP, TP, C), 1.0, 6.0, ((0, 16),))
    source_device_keys = jax.random.split(jax.random.fold_in(part_splits[1], 1), TILES * 8 // (8 * TILES_DEV))
    source_device_turns = jax.random.permutation(jax.random.fold_in(part_splits[1], 3), TILES * 8 // (8 * TILES_DEV))
    source_device = jax.vmap(lambda own, number: deal_out(jax.random.fold_in(part_splits[1], 2), own, number, 8 * TILES_DEV, N_TILE, 1, MOST, 1))(source_device_keys, source_device_turns).reshape((TILES, 8, 1))
    source_slot = set_ends(jax.random.randint(part_splits[2], (TILES, 8), 0, TILES_DEV), jax.random.fold_in(part_splits[2], 1), 0, TILES_DEV - 1).astype(jnp.int32)
    present = set_ends((jax.random.randint(part_splits[3], (TILES, 8), 0, 8) < 7).astype(jnp.int32), jax.random.fold_in(part_splits[3], 1), 0, 1)
    depth_kernel = draw_depth_kernel(jax.random.fold_in(key_list[9], 71), part)
    norm_gain = jnp.clip(1.0 + 0.18 * jax.random.normal(key_list[5], (NB, C), jnp.float32), 0.1, 1.9)
    w_in = noise(key_list[6], (NB, C, H), C ** -0.5, 0.375)
    w_out = noise(key_list[7], (NB, H, C), H ** -0.5, 0.1875)
    cotangent = gaussian_with(part_splits[8], (TILES, TP, TP, C), 1.0, 6.0, ((0, 16),), (0, 3, 16, 2.0))
    return {"tiles": tiles, "source_device": source_device, "source_slot": source_slot, "present": present, "depth_kernel": depth_kernel, "norm_gain": norm_gain, "w_in": w_in, "w_out": w_out, "cotangent": cotangent}


STRIP_KINDS = (1, 0, 3, 2, 1, 1, 0, 0)
NORM_EPSILON = 1e-06
ROOT_HALF = 0.7071067811865476
INV_ROOT_TWO_PI = 0.3989422804014327

def gelu_value(values):
    return values * 0.5 * (1.0 + lax.erf(values * ROOT_HALF))

def gelu_slope(values):
    return 0.5 * (1.0 + lax.erf(values * ROOT_HALF)) + values * INV_ROOT_TWO_PI * jnp.exp(-0.5 * values * values)

def strips_of(inputs):
    top_rows = inputs[:, 0:3]
    bottom_rows = inputs[:, -3:]
    left_cols = jnp.swapaxes(inputs[:, :, 0:3], 1, 2)
    right_cols = jnp.swapaxes(inputs[:, :, -3:], 1, 2)
    return jnp.stack([top_rows, bottom_rows, left_cols, right_cols], axis=1)

def strips_back(gradients, base):
    base = base.at[:, 0:3].add(gradients[:, 0])
    base = base.at[:, -3:].add(gradients[:, 1])
    base = base.at[:, :, 0:3].add(jnp.swapaxes(gradients[:, 2], 1, 2))
    base = base.at[:, :, -3:].add(jnp.swapaxes(gradients[:, 3], 1, 2))
    return base

def assemble(inputs, pieces):
    extent = inputs.shape[1]
    western = jnp.swapaxes(pieces[:, 2], 1, 2)
    eastern = jnp.swapaxes(pieces[:, 3], 1, 2)
    middle = jnp.concatenate([western, inputs, eastern], axis=2)
    upper = jnp.concatenate([pieces[:, 4, :, extent - 3:], pieces[:, 0], pieces[:, 5, :, 0:3]], axis=2)
    lower = jnp.concatenate([pieces[:, 6, :, extent - 3:], pieces[:, 1], pieces[:, 7, :, 0:3]], axis=2)
    return jnp.concatenate([upper, middle, lower], axis=1)

def disassemble(gradient):
    extent = gradient.shape[1] - 6
    centre = gradient[:, 3:extent + 3, 3:extent + 3]
    north = gradient[:, 0:3, 3:extent + 3]
    south = gradient[:, extent + 3:, 3:extent + 3]
    western = jnp.swapaxes(gradient[:, 3:extent + 3, 0:3], 1, 2)
    eastern = jnp.swapaxes(gradient[:, 3:extent + 3, extent + 3:], 1, 2)
    padding = jnp.zeros_like(gradient[:, 0:3, 0:extent - 3])
    north_west = jnp.concatenate([padding, gradient[:, 0:3, 0:3]], axis=2)
    north_east = jnp.concatenate([gradient[:, 0:3, extent + 3:], padding], axis=2)
    south_west = jnp.concatenate([padding, gradient[:, extent + 3:, 0:3]], axis=2)
    south_east = jnp.concatenate([gradient[:, extent + 3:, extent + 3:], padding], axis=2)
    stacked = jnp.stack([north, south, western, eastern, north_west, north_east, south_west, south_east], axis=1)
    return (centre, stacked)

def depthwise(padded, kernel):
    extent = padded.shape[1] - 6
    widened = padded.astype(jnp.float32)
    summed = jnp.zeros((padded.shape[0], extent, extent, padded.shape[3]), jnp.float32)
    for tap_row in range(7):
        for tap_col in range(7):
            summed = summed + widened[:, tap_row:tap_row + extent, tap_col:tap_col + extent] * kernel[7 * tap_row + tap_col]
    return summed

def depthwise_back(padded, kernel, back_conv):
    extent = back_conv.shape[1]
    widened = padded.astype(jnp.float32)
    back_pad = jnp.zeros(padded.shape, jnp.float32)
    tap_sums = []
    for tap_row in range(7):
        for tap_col in range(7):
            weighted = back_conv * kernel[7 * tap_row + tap_col]
            back_pad = back_pad + jnp.pad(weighted, ((0, 0), (tap_row, 6 - tap_row), (tap_col, 6 - tap_col), (0, 0)))
            window = widened[:, tap_row:tap_row + extent, tap_col:tap_col + extent]
            tap_sums.append(lax.optimization_barrier(jnp.sum(window * back_conv, axis=(0, 1, 2))))
    return (back_pad, jnp.stack(tap_sums))

def normalize(conv, gain):
    average = lax.optimization_barrier(jnp.mean(conv, axis=-1, keepdims=True))
    centred = conv - average
    spread = lax.optimization_barrier(jnp.mean(centred * centred, axis=-1, keepdims=True))
    inverse = lax.rsqrt(spread + NORM_EPSILON)
    unit = centred * inverse
    return (unit, inverse, (unit * gain).astype(jnp.bfloat16))

def gather_pieces(inputs, strip_index, present_mask):
    table = strips_of(inputs).reshape((-1, 3) + inputs.shape[2:])
    return jnp.take(table, strip_index, axis=0) * present_mask

def reference(tiles, source_device, source_slot, present, depth_kernel, norm_gain, w_in, w_out, cotangent):
    extent = tiles.shape[1]
    source = (source_device[:, :, 0] * TILES_DEV + source_slot).astype(jnp.int32)
    strip_index = (source * 4 + jnp.asarray(STRIP_KINDS, jnp.int32)[None, :]).astype(jnp.int32)
    present_mask = present.astype(jnp.bfloat16)[:, :, None, None, None]
    scale = 1.0 / math.sqrt(PIXELS)
    saved = []
    current = tiles
    for layer_index in range(NB):
        pieces = gather_pieces(current, strip_index, present_mask)
        padded = assemble(current, pieces)
        unit, inverse, normed = normalize(depthwise(padded, depth_kernel[layer_index]), norm_gain[layer_index])

        def mixing(row_group, weight_in=w_in[layer_index], weight_out=w_out[layer_index]):
            pre = jnp.dot(row_group, weight_in, preferred_element_type=jnp.float32)
            hidden = gelu_value(pre).astype(jnp.bfloat16)
            return jnp.dot(hidden, weight_out, preferred_element_type=jnp.float32)
        mixed = lax.map(mixing, normed.reshape(N_TILE, -1, C)).reshape(current.shape)
        saved.append((current, padded, unit, inverse, normed))
        current = (current.astype(jnp.float32) + mixed).astype(jnp.bfloat16)
    gradient = cotangent.astype(jnp.float32)
    grads_in = [None] * NB
    grads_out = [None] * NB
    grads_kernel = [None] * NB
    grads_gain = [None] * NB
    for layer_index in reversed(range(NB)):
        inputs, padded, unit, inverse, normed = saved[layer_index]
        rounded = gradient.astype(jnp.bfloat16)

        def accumulate(carry, group, weight_in=w_in[layer_index], weight_out=w_out[layer_index]):
            row_group, back_group = group
            pre = jnp.dot(row_group, weight_in, preferred_element_type=jnp.float32)
            hidden = gelu_value(pre).astype(jnp.bfloat16)
            back_hidden = jnp.dot(back_group, weight_out.T, preferred_element_type=jnp.float32)
            slope = (back_hidden * gelu_slope(pre)).astype(jnp.bfloat16)
            back_norm = jnp.dot(slope, weight_in.T, preferred_element_type=jnp.float32)
            first_sum = carry[0] + jnp.dot(row_group.T, slope, preferred_element_type=jnp.float32)
            second_sum = carry[1] + jnp.dot(back_group.T, hidden, preferred_element_type=jnp.float32)
            return ((first_sum, second_sum), back_norm)
        start_sums = (jnp.zeros((C, H), jnp.float32), jnp.zeros((C, H), jnp.float32))
        groups = (normed.reshape(N_TILE, -1, C), rounded.reshape(N_TILE, -1, C))
        (first_sum, second_sum), back_norm = lax.scan(accumulate, start_sums, groups)
        grads_in[layer_index] = first_sum
        grads_out[layer_index] = second_sum
        back_norm = back_norm.reshape(inputs.shape)
        scaled_back = back_norm * norm_gain[layer_index]
        grads_gain[layer_index] = lax.optimization_barrier(jnp.sum(back_norm * unit, axis=(0, 1, 2)))
        first_mean = lax.optimization_barrier(jnp.mean(scaled_back, axis=-1, keepdims=True))
        second_mean = lax.optimization_barrier(jnp.mean(scaled_back * unit, axis=-1, keepdims=True))
        back_conv = inverse * (scaled_back - first_mean - unit * second_mean)
        back_pad, grads_kernel[layer_index] = depthwise_back(padded, depth_kernel[layer_index], back_conv)
        centre, back_pieces = disassemble(back_pad)
        sending = lax.optimization_barrier((back_pieces * present_mask).astype(jnp.bfloat16)).astype(jnp.float32)
        table = jax.ops.segment_sum(sending.reshape((-1, 3) + inputs.shape[2:]), strip_index.reshape(-1), num_segments=TILES * 4)
        gradient = strips_back(table.reshape((TILES, 4, 3) + inputs.shape[2:]), gradient + centre)
    grad_tiles = gradient.astype(jnp.bfloat16)
    grad_in = jnp.stack(grads_in, axis=1) * scale
    grad_out = jnp.stack(grads_out, axis=1) * scale
    grad_kernel = jnp.stack(grads_kernel) * scale
    grad_gain = jnp.stack(grads_gain) * scale
    return (grad_tiles, grad_in, grad_out, grad_kernel, grad_gain)
```

```python
import math

import jax
import jax.numpy as jnp
from jax import lax
from jax.sharding import PartitionSpec as P

STRIP_KINDS = (1, 0, 3, 2, 1, 1, 0, 0)
NORM_EPSILON = 1e-06
ROOT_HALF = 0.7071067811865476
INV_ROOT_TWO_PI = 0.3989422804014327


def gelu_value(values):
    return values * 0.5 * (1.0 + lax.erf(values * ROOT_HALF))


def gelu_slope(values):
    return 0.5 * (1.0 + lax.erf(values * ROOT_HALF)) + values * INV_ROOT_TWO_PI * jnp.exp(
        -0.5 * values * values
    )


def strips_of(inputs):
    top_rows = inputs[:, 0:3]
    bottom_rows = inputs[:, -3:]
    left_cols = jnp.swapaxes(inputs[:, :, 0:3], 1, 2)
    right_cols = jnp.swapaxes(inputs[:, :, -3:], 1, 2)
    return jnp.stack([top_rows, bottom_rows, left_cols, right_cols], axis=1)


def strips_back(gradients, base):
    base = base.at[:, 0:3].add(gradients[:, 0])
    base = base.at[:, -3:].add(gradients[:, 1])
    base = base.at[:, :, 0:3].add(jnp.swapaxes(gradients[:, 2], 1, 2))
    base = base.at[:, :, -3:].add(jnp.swapaxes(gradients[:, 3], 1, 2))
    return base


def assemble(inputs, pieces):
    extent = inputs.shape[1]
    western = jnp.swapaxes(pieces[:, 2], 1, 2)
    eastern = jnp.swapaxes(pieces[:, 3], 1, 2)
    middle = jnp.concatenate([western, inputs, eastern], axis=2)
    upper = jnp.concatenate(
        [pieces[:, 4, :, extent - 3 :], pieces[:, 0], pieces[:, 5, :, 0:3]], axis=2
    )
    lower = jnp.concatenate(
        [pieces[:, 6, :, extent - 3 :], pieces[:, 1], pieces[:, 7, :, 0:3]], axis=2
    )
    return jnp.concatenate([upper, middle, lower], axis=1)


def disassemble(gradient):
    extent = gradient.shape[1] - 6
    centre = gradient[:, 3 : extent + 3, 3 : extent + 3]
    north = gradient[:, 0:3, 3 : extent + 3]
    south = gradient[:, extent + 3 :, 3 : extent + 3]
    western = jnp.swapaxes(gradient[:, 3 : extent + 3, 0:3], 1, 2)
    eastern = jnp.swapaxes(gradient[:, 3 : extent + 3, extent + 3 :], 1, 2)
    padding = jnp.zeros_like(gradient[:, 0:3, 0 : extent - 3])
    north_west = jnp.concatenate([padding, gradient[:, 0:3, 0:3]], axis=2)
    north_east = jnp.concatenate([gradient[:, 0:3, extent + 3 :], padding], axis=2)
    south_west = jnp.concatenate([padding, gradient[:, extent + 3 :, 0:3]], axis=2)
    south_east = jnp.concatenate([gradient[:, extent + 3 :, extent + 3 :], padding], axis=2)
    stacked = jnp.stack(
        [north, south, western, eastern, north_west, north_east, south_west, south_east], axis=1
    )
    return (centre, stacked)


def depthwise(padded, kernel):
    extent = padded.shape[1] - 6
    widened = padded.astype(jnp.float32)
    summed = jnp.zeros((padded.shape[0], extent, extent, padded.shape[3]), jnp.float32)
    for tap_row in range(7):
        for tap_col in range(7):
            summed = (
                summed
                + widened[:, tap_row : tap_row + extent, tap_col : tap_col + extent]
                * kernel[7 * tap_row + tap_col]
            )
    return summed


def depthwise_back(padded, kernel, back_conv):
    extent = back_conv.shape[1]
    wide_extent = extent + 6
    widened = padded.astype(jnp.float32)
    border = jnp.pad(back_conv, ((0, 0), (6, 6), (6, 6), (0, 0)))
    back_pad = jnp.zeros(padded.shape, jnp.float32)
    tap_sums = []
    for tap_row in range(7):
        for tap_col in range(7):
            shifted = border[
                :, 6 - tap_row : 6 - tap_row + wide_extent, 6 - tap_col : 6 - tap_col + wide_extent
            ]
            back_pad = back_pad + shifted * kernel[7 * tap_row + tap_col]
            window = widened[:, tap_row : tap_row + extent, tap_col : tap_col + extent]
            tap_sums.append(jnp.sum(window * back_conv, axis=(0, 1, 2)))
    return (back_pad, jnp.stack(tap_sums))


def normalize(conv, gain):
    average = jnp.mean(conv, axis=-1, keepdims=True)
    centred = conv - average
    spread = jnp.mean(centred * centred, axis=-1, keepdims=True)
    inverse = lax.rsqrt(spread + NORM_EPSILON)
    unit = centred * inverse
    return (unit, inverse, (unit * gain).astype(jnp.bfloat16))


def build_routes(source_device, source_slot, peers, capacity):
    row_total = source_slot.shape[0] * source_slot.shape[1]
    owner = source_device.reshape(row_total)
    codes = (source_slot * 4 + jnp.asarray(STRIP_KINDS, jnp.int32)[None, :]).reshape(row_total)
    later_rows = lax.broadcasted_iota(jnp.int32, (row_total, row_total), 0)
    other_rows = lax.broadcasted_iota(jnp.int32, (row_total, row_total), 1)
    before = jnp.logical_and(owner[:, None] == owner[None, :], other_rows < later_rows)
    ranking = jnp.sum(before.astype(jnp.int32), axis=1)
    slot_index = owner * capacity + ranking
    places = lax.broadcasted_iota(jnp.int32, (peers * capacity, row_total), 0)
    matched = (places == slot_index[None, :]).astype(jnp.int32)
    request = jnp.sum(matched * (codes[None, :] + 1), axis=1) - 1
    return (slot_index, request.reshape(peers, capacity))


def serve(inputs, wanted):
    table = strips_of(inputs).reshape((-1, 3) + inputs.shape[2:])
    rows = lax.broadcasted_iota(jnp.int32, wanted.shape + table.shape[:1], 2)
    chooser = (rows == wanted[:, :, None]).astype(inputs.dtype)
    return jnp.einsum("pks,sabc->pkabc", chooser, table)


def receive(incoming, slot_index, present_mask):
    flat = incoming.reshape((-1,) + incoming.shape[2:])
    rows = lax.broadcasted_iota(jnp.int32, slot_index.shape + flat.shape[:1], 1)
    chosen = (rows == slot_index[:, None]).astype(flat.dtype)
    chooser = chosen.reshape(present_mask.shape[:2] + flat.shape[:1]) * present_mask[:, :, 0, 0]
    return jnp.einsum("tds,sabc->tdabc", chooser, flat)


def pair_term(operand_set):
    row_block, slope, rounded, hidden = operand_set
    dims_rows = (((0,), (0,)), ((), ()))
    first_term = lax.dot_general(row_block, slope, dims_rows, preferred_element_type=jnp.float32)
    second_term = lax.dot_general(rounded, hidden, dims_rows, preferred_element_type=jnp.float32)
    return jnp.stack([first_term, second_term], axis=1)


def halve(values, steps):
    index = lax.axis_index("tile")
    peers = 1 << steps
    values = values.reshape((peers, -1) + values.shape[1:])
    for step in range(steps):
        pairs = values.reshape((-1, 2) + values.shape[1:])
        bit = (index >> step) & 1
        kept = jnp.where(bit == 1, pairs[:, 1], pairs[:, 0])
        sent = jnp.where(bit == 1, pairs[:, 0], pairs[:, 1]).astype(jnp.bfloat16)
        partners = [(place, place ^ (1 << step)) for place in range(peers)]
        values = kept + lax.ppermute(sent, "tile", partners).astype(jnp.float32)
    return values[0]


def double(values, steps):
    peers = 1 << steps
    for step in range(steps):
        partners = [(place, place ^ (1 << step)) for place in range(peers)]
        values = values + lax.ppermute(values, "tile", partners)
    return values


def body(
    tiles, source_device, source_slot, present, depth_kernel, norm_gain, w_in, w_out, cotangent
):
    peers = lax.axis_size("tile")
    local_tiles = tiles.shape[0]
    extent = tiles.shape[1]
    channels = tiles.shape[3]
    layers = w_in.shape[0]
    capacity = max(2, 2 * ((8 * local_tiles + peers - 1) // peers))
    scale = 1.0 / math.sqrt(local_tiles * peers * extent * extent)
    slot_index, request = build_routes(source_device, source_slot, peers, capacity)
    wanted = lax.all_to_all(request, "tile", split_axis=0, concat_axis=0, tiled=True)
    present_mask = present.astype(jnp.bfloat16)[:, :, None, None, None]
    dims_cols = (((1,), (1,)), ((), ()))
    saved = []
    current = tiles
    for layer_index in range(layers):
        incoming = lax.all_to_all(
            serve(current, wanted), "tile", split_axis=0, concat_axis=0, tiled=True
        )
        padded = assemble(current, receive(incoming, slot_index, present_mask))
        unit, inverse, normed = normalize(
            depthwise(padded, depth_kernel[layer_index]), norm_gain[layer_index]
        )
        row_block = normed.reshape(-1, channels)
        pre = jnp.dot(row_block, w_in[layer_index], preferred_element_type=jnp.float32)
        hidden = gelu_value(pre).astype(jnp.bfloat16)
        mixed = jnp.dot(hidden, w_out[layer_index], preferred_element_type=jnp.float32)
        kept = padded
        saved.append(
            (
                current,
                kept,
                unit.reshape(-1, channels),
                inverse.reshape(-1, 1),
                row_block,
                pre,
                hidden,
            )
        )
        current = (current.astype(jnp.float32) + mixed.reshape(current.shape)).astype(jnp.bfloat16)
    gradient = cotangent.astype(jnp.float32)
    weight_terms = [None] * layers
    small_terms = [None] * layers
    steps = peers.bit_length() - 1
    for layer_index in reversed(range(layers)):
        inputs, kept, unit, inverse, row_block, pre, hidden = saved[layer_index]
        rounded = gradient.astype(jnp.bfloat16).reshape(-1, channels)
        back_hidden = lax.dot_general(
            rounded, w_out[layer_index], dims_cols, preferred_element_type=jnp.float32
        )
        slope = (back_hidden * gelu_slope(pre)).astype(jnp.bfloat16)
        back_norm = lax.dot_general(
            slope, w_in[layer_index], dims_cols, preferred_element_type=jnp.float32
        )
        operand_set = (row_block, slope, rounded, hidden)
        weight_terms[layer_index] = halve(pair_term(operand_set), steps)
        scaled_back = back_norm * norm_gain[layer_index]
        gain_term = jnp.sum(back_norm * unit, axis=0)
        first_mean = jnp.mean(scaled_back, axis=-1, keepdims=True)
        second_mean = jnp.mean(scaled_back * unit, axis=-1, keepdims=True)
        back_conv = (inverse * (scaled_back - first_mean - unit * second_mean)).reshape(
            inputs.shape
        )
        padded = kept
        back_pad, kernel_term = depthwise_back(padded, depth_kernel[layer_index], back_conv)
        small_terms[layer_index] = double(
            jnp.concatenate([kernel_term, gain_term[None]], axis=0), steps
        )
        centre, back_pieces = disassemble(back_pad)
        sending = (back_pieces * present_mask).astype(jnp.bfloat16)
        piece_shape = sending.shape[2:]
        places = lax.broadcasted_iota(jnp.int32, (peers * capacity,) + slot_index.shape, 0)
        spread = (places == slot_index[None]).astype(jnp.bfloat16)
        outgoing = jnp.einsum(
            "sr,rabc->sabc", spread, sending.reshape((-1,) + piece_shape)
        )
        returned = lax.all_to_all(
            outgoing.reshape((peers, capacity) + piece_shape),
            "tile",
            split_axis=0,
            concat_axis=0,
            tiled=True,
        )
        strip_codes = lax.broadcasted_iota(jnp.int32, (local_tiles * 4, peers * capacity), 0)
        chooser = (strip_codes == wanted.reshape(1, -1)).astype(jnp.bfloat16)
        collected = jnp.dot(
            chooser, returned.reshape(peers * capacity, -1), preferred_element_type=jnp.float32
        )
        gradient = strips_back(collected.reshape((local_tiles, 4) + piece_shape), gradient + centre)
    weights_part = jnp.stack(weight_terms, axis=2)
    small = jnp.stack(small_terms)
    kernel_sum, gain_sum = small[:, :-1], small[:, -1]
    grad_tiles = gradient.astype(jnp.bfloat16)
    return (
        grad_tiles,
        weights_part[:, 0] * scale,
        weights_part[:, 1] * scale,
        kernel_sum * scale,
        gain_sum * scale,
    )


def solution(mesh):
    return jax.shard_map(
        body,
        mesh=mesh,
        in_specs=(
            P(("parts", "tile"), None, None, None),
            P(("parts", "tile"), None, None),
            P(("parts", "tile"), None),
            P(("parts", "tile"), None),
            P(),
            P(),
            P(),
            P(),
            P(("parts", "tile"), None, None, None),
        ),
        out_specs=(
            P(("parts", "tile"), None, None, None),
            P(("parts", "tile"), None, None),
            P(("parts", "tile"), None, None),
            P("parts", None, None),
            P("parts", None),
        ),
        check_vma=False,
    )
```

```python
import math

import jax
import jax.numpy as jnp
from jax import lax
from jax.experimental import pallas as pl
from jax.experimental.pallas import tpu as pltpu
from jax.sharding import PartitionSpec as P

STRIP_KINDS = (1, 0, 3, 2, 1, 1, 0, 0)
NORM_EPSILON = 1e-06
ROOT_HALF = 0.7071067811865476
INV_ROOT_TWO_PI = 0.3989422804014327


def gelu_value(values):
    return values * 0.5 * (1.0 + lax.erf(values * ROOT_HALF))


def gelu_slope(values):
    return 0.5 * (1.0 + lax.erf(values * ROOT_HALF)) + values * INV_ROOT_TWO_PI * jnp.exp(
        -0.5 * values * values
    )


LANES = 128
SMEM = pl.BlockSpec(memory_space=pltpu.SMEM)
VMEM = pl.BlockSpec(memory_space=pltpu.VMEM)


def serve_kernel(wanted_ref, inputs_ref, out_ref, wide_ref, table_ref):
    for tile in range(inputs_ref.shape[0]):
        wide_ref[...] = inputs_ref[tile].astype(jnp.float32)
        table_ref[4 * tile] = wide_ref[0:3]
        table_ref[4 * tile + 1] = wide_ref[13:16]
        for depth in range(3):
            for place in range(16):
                row = pl.ds(place, 1)
                table_ref[4 * tile + 2, depth, row] = wide_ref[place, pl.ds(depth, 1)]
                table_ref[4 * tile + 3, depth, row] = wide_ref[place, pl.ds(13 + depth, 1)]

    def one(slot, carry):
        code = wanted_ref[slot]
        strip = table_ref[jnp.maximum(code, 0)]
        out_ref[slot] = jnp.where(code >= 0, strip, 0.0).astype(out_ref.dtype)
        return carry

    lax.fori_loop(0, out_ref.shape[0], one, 0)


def serve(inputs, wanted):
    tiles, extent, _, channels = inputs.shape
    return pl.pallas_call(
        serve_kernel,
        out_shape=jax.ShapeDtypeStruct((wanted.shape[0], 3, extent, channels), jnp.bfloat16),
        in_specs=[SMEM, VMEM],
        out_specs=VMEM,
        scratch_shapes=[
            pltpu.VMEM((extent, extent, channels), jnp.float32),
            pltpu.VMEM((4 * tiles, 3, extent, channels), jnp.float32),
        ],
        compiler_params=pltpu.CompilerParams(vmem_limit_bytes=32 * 1024 * 1024),
        name="serve",
    )(wanted, inputs)


def shift_columns(padded_ref, tile, shifted_ref):
    for tap_col in range(7):
        shifted_ref[tap_col] = padded_ref[tile, :, tap_col : tap_col + 16, :]


def forward_kernel(
    slot_ref, present_ref, inputs_ref, incoming_ref, kernel_ref, padded_ref, conv_ref, piece_ref, shifted_ref
):
    for tile in range(inputs_ref.shape[0]):

        def piece(direction):
            row = 8 * tile + direction
            strip = incoming_ref[slot_ref[row]].astype(jnp.float32)
            return jnp.where(present_ref[row] > 0, strip, 0.0)

        padded_ref[tile, 3:19, 3:19, :] = inputs_ref[tile].astype(jnp.float32)
        padded_ref[tile, 0:3, 3:19, :] = piece(0)
        padded_ref[tile, 19:22, 3:19, :] = piece(1)
        for direction, first in ((2, 0), (3, 19)):
            piece_ref[...] = piece(direction)
            for depth in range(3):
                for place in range(16):
                    padded_ref[tile, 3 + place, pl.ds(first + depth, 1)] = piece_ref[
                        depth, pl.ds(place, 1)
                    ]
        for direction, top, left, taken in ((4, 0, 0, 13), (5, 0, 19, 0), (6, 19, 0, 13), (7, 19, 19, 0)):
            piece_ref[...] = piece(direction)
            padded_ref[tile, top : top + 3, left : left + 3, :] = piece_ref[:, taken : taken + 3, :]
        padded_ref[tile, :, 22:24, :] = jnp.zeros((22, 2, padded_ref.shape[3]), jnp.float32)
        shift_columns(padded_ref, tile, shifted_ref)
        for half in range(conv_ref.shape[3] // LANES):
            lanes = pl.ds(half * LANES, LANES)

            def rows(step, carry):
                top = step * 4
                sums = [jnp.zeros((16, LANES), jnp.float32)] * 4
                for tap_col in range(7):
                    window = [shifted_ref[tap_col, top + row, :, lanes] for row in range(10)]
                    for tap_row in range(7):
                        weight = kernel_ref[pl.ds(7 * tap_row + tap_col, 1), lanes]
                        sums = [sums[row] + window[row + tap_row] * weight for row in range(4)]
                for row in range(4):
                    conv_ref[tile, top + row, :, lanes] = sums[row]
                return carry

            lax.fori_loop(0, 4, rows, 0)


def forward_conv(inputs, incoming, slot_index, present, kernel):
    tiles, extent, _, channels = inputs.shape
    return pl.pallas_call(
        forward_kernel,
        out_shape=(
            jax.ShapeDtypeStruct((tiles, extent + 6, extent + 8, channels), jnp.float32),
            jax.ShapeDtypeStruct((tiles, extent, extent, channels), jnp.float32),
        ),
        in_specs=[SMEM, SMEM, VMEM, VMEM, VMEM],
        out_specs=(VMEM, VMEM),
        scratch_shapes=[
            pltpu.VMEM((3, extent, channels), jnp.float32),
            pltpu.VMEM((7, extent + 6, extent, channels), jnp.float32),
        ],
        compiler_params=pltpu.CompilerParams(vmem_limit_bytes=32 * 1024 * 1024),
        name="forward_conv",
    )(slot_index, present, inputs, incoming, kernel)


def backward_kernel(
    slot_ref, present_ref, padded_ref, slopes_ref, kernel_ref,
    centre_ref, outgoing_ref, taps_ref, piece_ref, shifted_ref, border_ref, sums_ref, back_ref,
):
    channels = slopes_ref.shape[3]
    outgoing_ref[...] = jnp.zeros(outgoing_ref.shape, outgoing_ref.dtype)
    border_ref[...] = jnp.zeros(border_ref.shape, jnp.float32)
    for tile in range(slopes_ref.shape[0]):
        shift_columns(padded_ref, tile, shifted_ref)
        for tap_col in range(7):
            border_ref[tap_col, 6:22, tap_col : tap_col + 16, :] = slopes_ref[tile]
        for half in range(channels // LANES):
            lanes = pl.ds(half * LANES, LANES)

            def taps(tap_col, carry):
                def rows(step, sums):
                    top = step * 4
                    slopes = [slopes_ref[tile, top + row, :, lanes] for row in range(4)]
                    window = [shifted_ref[tap_col, top + row, :, lanes] for row in range(10)]
                    return tuple(
                        sums[tap_row]
                        + (
                            window[tap_row] * slopes[0]
                            + window[tap_row + 1] * slopes[1]
                            + window[tap_row + 2] * slopes[2]
                            + window[tap_row + 3] * slopes[3]
                        )
                        for tap_row in range(7)
                    )

                sums = lax.fori_loop(0, 4, rows, (jnp.zeros((16, LANES), jnp.float32),) * 7)
                for tap_row in range(7):
                    if tile == 0:
                        sums_ref[tap_col, tap_row, :, lanes] = sums[tap_row]
                    else:
                        sums_ref[tap_col, tap_row, :, lanes] += sums[tap_row]
                return carry

            lax.fori_loop(0, 7, taps, 0)

            def rows_back(step, carry):
                top = step * 2
                sums = [jnp.zeros((24, LANES), jnp.float32)] * 2
                for tap_col in range(7):
                    window = [border_ref[tap_col, top + row, :, lanes] for row in range(8)]
                    for tap_row in range(7):
                        weight = kernel_ref[pl.ds(7 * tap_row + tap_col, 1), lanes]
                        sums = [sums[row] + window[row + 6 - tap_row] * weight for row in range(2)]
                for row in range(2):
                    back_ref[top + row, :, lanes] = sums[row]
                return carry

            lax.fori_loop(0, 11, rows_back, 0)

        centre_ref[tile] = back_ref[3:19, 3:19, :]

        def send(direction):
            row = 8 * tile + direction
            strip = jnp.where(present_ref[row] > 0, piece_ref[...], 0.0)
            outgoing_ref[slot_ref[row]] = strip.astype(outgoing_ref.dtype)

        piece_ref[...] = back_ref[0:3, 3:19, :]
        send(0)
        piece_ref[...] = back_ref[19:22, 3:19, :]
        send(1)
        for direction, first in ((2, 0), (3, 19)):
            for depth in range(3):
                for place in range(16):
                    piece_ref[depth, pl.ds(place, 1)] = back_ref[
                        3 + place, pl.ds(first + depth, 1)
                    ]
            send(direction)
        for direction, top, left, taken in ((4, 0, 0, 13), (5, 0, 19, 0), (6, 19, 0, 13), (7, 19, 19, 0)):
            piece_ref[...] = jnp.zeros(piece_ref.shape, jnp.float32)
            piece_ref[:, taken : taken + 3, :] = back_ref[top : top + 3, left : left + 3, :]
            send(direction)
    for tap_col in range(7):
        for tap_row in range(7):
            taps_ref[pl.ds(7 * tap_row + tap_col, 1)] = jnp.sum(
                sums_ref[tap_col, tap_row], axis=0, keepdims=True
            )


def backward_conv(padded, back_conv, slot_index, present, kernel, slots):
    tiles, extent, _, channels = back_conv.shape
    return pl.pallas_call(
        backward_kernel,
        out_shape=(
            jax.ShapeDtypeStruct(back_conv.shape, jnp.float32),
            jax.ShapeDtypeStruct((slots, 3, extent, channels), jnp.bfloat16),
            jax.ShapeDtypeStruct((49, channels), jnp.float32),
        ),
        in_specs=[SMEM, SMEM, VMEM, VMEM, VMEM],
        out_specs=(VMEM, VMEM, VMEM),
        scratch_shapes=[
            pltpu.VMEM((3, extent, channels), jnp.float32),
            pltpu.VMEM((7, extent + 6, extent, channels), jnp.float32),
            pltpu.VMEM((7, extent + 12, extent + 8, channels), jnp.float32),
            pltpu.VMEM((7, 7, extent, channels), jnp.float32),
            pltpu.VMEM((extent + 6, extent + 8, channels), jnp.float32),
        ],
        compiler_params=pltpu.CompilerParams(vmem_limit_bytes=48 * 1024 * 1024),
        name="backward_conv",
    )(slot_index, present, padded, back_conv, kernel)


def collect_kernel(wanted_ref, base_ref, centre_ref, returned_ref, out_ref, table_ref):
    table_ref[...] = jnp.zeros(table_ref.shape, jnp.float32)

    def one(slot, carry):
        code = wanted_ref[slot]
        strip = returned_ref[slot].astype(jnp.float32)
        table_ref[jnp.maximum(code, 0)] += jnp.where(code >= 0, strip, 0.0)
        return carry

    lax.fori_loop(0, returned_ref.shape[0], one, 0)
    for tile in range(base_ref.shape[0]):
        out_ref[tile] = base_ref[tile].astype(jnp.float32) + centre_ref[tile]
        out_ref[tile, 0:3] += table_ref[4 * tile]
        out_ref[tile, 13:16] += table_ref[4 * tile + 1]
        for depth in range(3):
            for place in range(16):
                row = pl.ds(place, 1)
                out_ref[tile, place, pl.ds(depth, 1)] += table_ref[4 * tile + 2, depth, row]
                out_ref[tile, place, pl.ds(13 + depth, 1)] += table_ref[4 * tile + 3, depth, row]


def collect(base, centre, returned, wanted):
    tiles, extent, _, channels = base.shape
    return pl.pallas_call(
        collect_kernel,
        out_shape=jax.ShapeDtypeStruct(base.shape, jnp.float32),
        in_specs=[SMEM, VMEM, VMEM, VMEM],
        out_specs=VMEM,
        scratch_shapes=[pltpu.VMEM((4 * tiles, 3, extent, channels), jnp.float32)],
        compiler_params=pltpu.CompilerParams(vmem_limit_bytes=32 * 1024 * 1024),
        name="collect",
    )(wanted, base, centre, returned)


def normalize(conv, gain):
    average = jnp.mean(conv, axis=-1, keepdims=True)
    centred = conv - average
    spread = jnp.mean(centred * centred, axis=-1, keepdims=True)
    inverse = lax.rsqrt(spread + NORM_EPSILON)
    unit = centred * inverse
    return (unit, inverse, (unit * gain).astype(jnp.bfloat16))


def build_routes(source_device, source_slot, peers, capacity):
    row_total = source_slot.shape[0] * source_slot.shape[1]
    owner = source_device.reshape(row_total)
    codes = (source_slot * 4 + jnp.asarray(STRIP_KINDS, jnp.int32)[None, :]).reshape(row_total)
    later_rows = lax.broadcasted_iota(jnp.int32, (row_total, row_total), 0)
    other_rows = lax.broadcasted_iota(jnp.int32, (row_total, row_total), 1)
    before = jnp.logical_and(owner[:, None] == owner[None, :], other_rows < later_rows)
    ranking = jnp.sum(before.astype(jnp.int32), axis=1)
    slot_index = owner * capacity + ranking
    places = lax.broadcasted_iota(jnp.int32, (peers * capacity, row_total), 0)
    matched = (places == slot_index[None, :]).astype(jnp.int32)
    request = jnp.sum(matched * (codes[None, :] + 1), axis=1) - 1
    return (slot_index, request.reshape(peers, capacity))


def pair_term(operand_set):
    row_block, slope, rounded, hidden = operand_set
    dims_rows = (((0,), (0,)), ((), ()))
    first_term = lax.dot_general(row_block, slope, dims_rows, preferred_element_type=jnp.float32)
    second_term = lax.dot_general(rounded, hidden, dims_rows, preferred_element_type=jnp.float32)
    return jnp.stack([first_term, second_term], axis=1)


def halve(values, steps):
    index = lax.axis_index("tile")
    peers = 1 << steps
    values = values.reshape((peers, -1) + values.shape[1:])
    for step in range(steps):
        pairs = values.reshape((-1, 2) + values.shape[1:])
        bit = (index >> step) & 1
        kept = jnp.where(bit == 1, pairs[:, 1], pairs[:, 0])
        sent = jnp.where(bit == 1, pairs[:, 0], pairs[:, 1]).astype(jnp.bfloat16)
        partners = [(place, place ^ (1 << step)) for place in range(peers)]
        values = kept + lax.ppermute(sent, "tile", partners).astype(jnp.float32)
    return values[0]


def double(values, steps):
    peers = 1 << steps
    for step in range(steps):
        partners = [(place, place ^ (1 << step)) for place in range(peers)]
        values = values + lax.ppermute(values, "tile", partners)
    return values


def exchange(blocks, peers):
    arranged = blocks.reshape((peers, -1) + blocks.shape[1:])
    returned = lax.all_to_all(arranged, "tile", split_axis=0, concat_axis=0, tiled=True)
    return returned.reshape(blocks.shape)


def body(
    tiles, source_device, source_slot, present, depth_kernel, norm_gain, w_in, w_out, cotangent
):
    peers = lax.axis_size("tile")
    local_tiles = tiles.shape[0]
    extent = tiles.shape[1]
    channels = tiles.shape[3]
    layers = w_in.shape[0]
    capacity = max(2, 2 * ((8 * local_tiles + peers - 1) // peers))
    scale = 1.0 / math.sqrt(local_tiles * peers * extent * extent)
    slot_index, request = build_routes(source_device, source_slot, peers, capacity)
    wanted = lax.all_to_all(request, "tile", split_axis=0, concat_axis=0, tiled=True).reshape(-1)
    present = present.reshape(-1)
    dims_cols = (((1,), (1,)), ((), ()))
    saved = []
    current = tiles
    for layer_index in range(layers):
        incoming = exchange(serve(current, wanted), peers)
        padded, conv = forward_conv(
            current, incoming, slot_index, present, depth_kernel[layer_index]
        )
        unit, inverse, normed = normalize(conv, norm_gain[layer_index])
        row_block = normed.reshape(-1, channels)
        pre = jnp.dot(row_block, w_in[layer_index], preferred_element_type=jnp.float32)
        hidden = gelu_value(pre).astype(jnp.bfloat16)
        mixed = jnp.dot(hidden, w_out[layer_index], preferred_element_type=jnp.float32)
        kept = padded
        saved.append(
            (
                current,
                kept,
                unit.reshape(-1, channels),
                inverse.reshape(-1, 1),
                row_block,
                pre,
                hidden,
            )
        )
        current = (current.astype(jnp.float32) + mixed.reshape(current.shape)).astype(jnp.bfloat16)
    gradient = cotangent.astype(jnp.float32)
    weight_terms = [None] * layers
    small_terms = [None] * layers
    steps = peers.bit_length() - 1
    for layer_index in reversed(range(layers)):
        inputs, kept, unit, inverse, row_block, pre, hidden = saved[layer_index]
        rounded = gradient.astype(jnp.bfloat16).reshape(-1, channels)
        back_hidden = lax.dot_general(
            rounded, w_out[layer_index], dims_cols, preferred_element_type=jnp.float32
        )
        slope = (back_hidden * gelu_slope(pre)).astype(jnp.bfloat16)
        back_norm = lax.dot_general(
            slope, w_in[layer_index], dims_cols, preferred_element_type=jnp.float32
        )
        operand_set = (row_block, slope, rounded, hidden)
        weight_terms[layer_index] = halve(pair_term(operand_set), steps)
        scaled_back = back_norm * norm_gain[layer_index]
        gain_term = jnp.sum(back_norm * unit, axis=0)
        first_mean = jnp.mean(scaled_back, axis=-1, keepdims=True)
        second_mean = jnp.mean(scaled_back * unit, axis=-1, keepdims=True)
        back_conv = (inverse * (scaled_back - first_mean - unit * second_mean)).reshape(
            inputs.shape
        )
        centre, outgoing, kernel_term = backward_conv(
            kept, back_conv, slot_index, present, depth_kernel[layer_index], peers * capacity
        )
        small_terms[layer_index] = double(
            jnp.concatenate([kernel_term, gain_term[None]], axis=0), steps
        )
        gradient = collect(gradient, centre, exchange(outgoing, peers), wanted)
    weights_part = jnp.stack(weight_terms, axis=2)
    small = jnp.stack(small_terms)
    kernel_sum, gain_sum = small[:, :-1], small[:, -1]
    grad_tiles = gradient.astype(jnp.bfloat16)
    return (
        grad_tiles,
        weights_part[:, 0] * scale,
        weights_part[:, 1] * scale,
        kernel_sum * scale,
        gain_sum * scale,
    )


def solution(mesh):
    return jax.shard_map(
        body,
        mesh=mesh,
        in_specs=(
            P(("parts", "tile"), None, None, None),
            P(("parts", "tile"), None, None),
            P(("parts", "tile"), None),
            P(("parts", "tile"), None),
            P(),
            P(),
            P(),
            P(),
            P(("parts", "tile"), None, None, None),
        ),
        out_specs=(
            P(("parts", "tile"), None, None, None),
            P(("parts", "tile"), None, None),
            P(("parts", "tile"), None, None),
            P("parts", None, None),
            P("parts", None),
        ),
        check_vma=False,
    )
```

```python
import functools
import math

import jax
import jax.numpy as jnp
from jax import lax
from jax.experimental import pallas as pl
from jax.experimental.pallas import tpu as pltpu
from jax.sharding import PartitionSpec as P

STRIP_KINDS = (1, 0, 3, 2, 1, 1, 0, 0)
NORM_EPSILON = 1e-06
ROOT_HALF = 0.7071067811865476
INV_ROOT_TWO_PI = 0.3989422804014327


def gelu_value(values):
    return values * 0.5 * (1.0 + lax.erf(values * ROOT_HALF))


def gelu_slope(values):
    return 0.5 * (1.0 + lax.erf(values * ROOT_HALF)) + values * INV_ROOT_TWO_PI * jnp.exp(
        -0.5 * values * values
    )


LANES = 128
SMEM = pl.BlockSpec(memory_space=pltpu.SMEM)
VMEM = pl.BlockSpec(memory_space=pltpu.VMEM)


def estimate(microseconds):
    return pl.CostEstimate(
        flops=int(microseconds * 1.1e9), bytes_accessed=int(microseconds * 3.6e6), transcendentals=0
    )


def exchange_kernel(peers, source_ref, target_ref, send_sem, recv_sem, own_sem):
    me = lax.axis_index("tile")
    barrier = pltpu.get_barrier_semaphore()

    def greet(offset, carry):
        pl.semaphore_signal(
            barrier,
            inc=1,
            device_id={"tile": lax.rem(me + offset, peers)},
            device_id_type=pl.DeviceIdType.MESH,
        )
        return carry

    def remote(offset):
        other = lax.rem(me + offset, peers)
        return pltpu.make_async_remote_copy(
            src_ref=source_ref.at[other],
            dst_ref=target_ref.at[me],
            send_sem=send_sem.at[offset],
            recv_sem=recv_sem.at[offset],
            device_id={"tile": other},
            device_id_type=pl.DeviceIdType.MESH,
        )

    def begin(offset, carry):
        remote(offset).start()
        return carry

    def finish(offset, carry):
        remote(offset).wait()
        return carry

    lax.fori_loop(1, peers, greet, 0)
    pl.semaphore_wait(barrier, peers - 1)
    lax.fori_loop(1, peers, begin, 0)
    own = pltpu.make_async_copy(source_ref.at[me], target_ref.at[me], own_sem)
    own.start()
    lax.fori_loop(1, peers, finish, 0)
    own.wait()


def direct_exchange(blocks, peers, identity):
    arranged = blocks.reshape((peers, -1) + blocks.shape[1:])
    returned = pl.pallas_call(
        functools.partial(exchange_kernel, peers),
        out_shape=jax.ShapeDtypeStruct(arranged.shape, arranged.dtype),
        in_specs=[VMEM],
        out_specs=VMEM,
        scratch_shapes=[
            pltpu.SemaphoreType.DMA((peers,)),
            pltpu.SemaphoreType.DMA((peers,)),
            pltpu.SemaphoreType.DMA,
        ],
        compiler_params=pltpu.CompilerParams(
            collective_id=identity, has_side_effects=True, vmem_limit_bytes=16 * 1024 * 1024
        ),
        name="exchange_requests" if identity == 0 else "exchange_strips",
    )(arranged)
    return returned.reshape(blocks.shape)


def serve_kernel(wanted_ref, inputs_ref, out_ref, wide_ref, table_ref):
    for tile in range(inputs_ref.shape[0]):
        wide_ref[...] = inputs_ref[tile].astype(jnp.float32)
        table_ref[4 * tile] = wide_ref[0:3]
        table_ref[4 * tile + 1] = wide_ref[13:16]
        for depth in range(3):
            for place in range(16):
                row = pl.ds(place, 1)
                table_ref[4 * tile + 2, depth, row] = wide_ref[place, pl.ds(depth, 1)]
                table_ref[4 * tile + 3, depth, row] = wide_ref[place, pl.ds(13 + depth, 1)]

    def one(slot, carry):
        code = wanted_ref[slot]
        strip = table_ref[jnp.maximum(code, 0)]
        out_ref[slot] = jnp.where(code >= 0, strip, 0.0).astype(out_ref.dtype)
        return carry

    lax.fori_loop(0, out_ref.shape[0], one, 0)


def serve(inputs, wanted):
    tiles, extent, _, channels = inputs.shape
    return pl.pallas_call(
        serve_kernel,
        out_shape=jax.ShapeDtypeStruct((wanted.shape[0], 3, extent, channels), jnp.bfloat16),
        in_specs=[SMEM, VMEM],
        out_specs=VMEM,
        scratch_shapes=[
            pltpu.VMEM((extent, extent, channels), jnp.float32),
            pltpu.VMEM((4 * tiles, 3, extent, channels), jnp.float32),
        ],
        compiler_params=pltpu.CompilerParams(vmem_limit_bytes=32 * 1024 * 1024),
        name="serve",
    )(wanted, inputs)


def shift_columns(padded_ref, tile, shifted_ref):
    for tap_col in range(7):
        shifted_ref[tap_col] = padded_ref[tile, :, tap_col : tap_col + 16, :]


def forward_kernel(
    slot_ref, present_ref, inputs_ref, incoming_ref, kernel_ref, padded_ref, conv_ref, piece_ref, shifted_ref
):
    for tile in range(inputs_ref.shape[0]):

        def piece(direction):
            row = 8 * tile + direction
            strip = incoming_ref[slot_ref[row]].astype(jnp.float32)
            return jnp.where(present_ref[row] > 0, strip, 0.0)

        padded_ref[tile, 3:19, 3:19, :] = inputs_ref[tile].astype(jnp.float32)
        padded_ref[tile, 0:3, 3:19, :] = piece(0)
        padded_ref[tile, 19:22, 3:19, :] = piece(1)
        for direction, first in ((2, 0), (3, 19)):
            piece_ref[...] = piece(direction)
            for depth in range(3):
                for place in range(16):
                    padded_ref[tile, 3 + place, pl.ds(first + depth, 1)] = piece_ref[
                        depth, pl.ds(place, 1)
                    ]
        for direction, top, left, taken in ((4, 0, 0, 13), (5, 0, 19, 0), (6, 19, 0, 13), (7, 19, 19, 0)):
            piece_ref[...] = piece(direction)
            padded_ref[tile, top : top + 3, left : left + 3, :] = piece_ref[:, taken : taken + 3, :]
        padded_ref[tile, :, 22:24, :] = jnp.zeros((22, 2, padded_ref.shape[3]), jnp.float32)
        shift_columns(padded_ref, tile, shifted_ref)
        for half in range(conv_ref.shape[3] // LANES):
            lanes = pl.ds(half * LANES, LANES)

            def rows(step, carry):
                top = step * 4
                sums = [jnp.zeros((16, LANES), jnp.float32)] * 4
                for tap_col in range(7):
                    window = [shifted_ref[tap_col, top + row, :, lanes] for row in range(10)]
                    for tap_row in range(7):
                        weight = kernel_ref[pl.ds(7 * tap_row + tap_col, 1), lanes]
                        sums = [sums[row] + window[row + tap_row] * weight for row in range(4)]
                for row in range(4):
                    conv_ref[tile, top + row, :, lanes] = sums[row]
                return carry

            lax.fori_loop(0, 4, rows, 0)


def forward_conv(inputs, incoming, slot_index, present, kernel):
    tiles, extent, _, channels = inputs.shape
    return pl.pallas_call(
        forward_kernel,
        out_shape=(
            jax.ShapeDtypeStruct((tiles, extent + 6, extent + 8, channels), jnp.float32),
            jax.ShapeDtypeStruct((tiles, extent, extent, channels), jnp.float32),
        ),
        in_specs=[SMEM, SMEM, VMEM, VMEM, VMEM],
        out_specs=(VMEM, VMEM),
        scratch_shapes=[
            pltpu.VMEM((3, extent, channels), jnp.float32),
            pltpu.VMEM((7, extent + 6, extent, channels), jnp.float32),
        ],
        compiler_params=pltpu.CompilerParams(vmem_limit_bytes=32 * 1024 * 1024),
        name="forward_conv",
    )(slot_index, present, inputs, incoming, kernel)


def taps_kernel(padded_ref, slopes_ref, taps_ref, shifted_ref, sums_ref):
    channels = slopes_ref.shape[3]
    for tile in range(slopes_ref.shape[0]):
        shift_columns(padded_ref, tile, shifted_ref)
        for half in range(channels // LANES):
            lanes = pl.ds(half * LANES, LANES)

            def taps(tap_col, carry):
                def rows(step, sums):
                    top = step * 4
                    slopes = [slopes_ref[tile, top + row, :, lanes] for row in range(4)]
                    window = [shifted_ref[tap_col, top + row, :, lanes] for row in range(10)]
                    return tuple(
                        sums[tap_row]
                        + (
                            window[tap_row] * slopes[0]
                            + window[tap_row + 1] * slopes[1]
                            + window[tap_row + 2] * slopes[2]
                            + window[tap_row + 3] * slopes[3]
                        )
                        for tap_row in range(7)
                    )

                sums = lax.fori_loop(0, 4, rows, (jnp.zeros((16, LANES), jnp.float32),) * 7)
                for tap_row in range(7):
                    if tile == 0:
                        sums_ref[tap_col, tap_row, :, lanes] = sums[tap_row]
                    else:
                        sums_ref[tap_col, tap_row, :, lanes] += sums[tap_row]
                return carry

            lax.fori_loop(0, 7, taps, 0)
    for tap_col in range(7):
        for tap_row in range(7):
            taps_ref[pl.ds(7 * tap_row + tap_col, 1)] = jnp.sum(
                sums_ref[tap_col, tap_row], axis=0, keepdims=True
            )


def tap_sums(padded, back_conv):
    _, extent, _, channels = back_conv.shape
    return pl.pallas_call(
        taps_kernel,
        out_shape=jax.ShapeDtypeStruct((49, channels), jnp.float32),
        in_specs=[VMEM, VMEM],
        out_specs=VMEM,
        scratch_shapes=[
            pltpu.VMEM((7, extent + 6, extent, channels), jnp.float32),
            pltpu.VMEM((7, 7, extent, channels), jnp.float32),
        ],
        compiler_params=pltpu.CompilerParams(vmem_limit_bytes=32 * 1024 * 1024),
        cost_estimate=estimate(5),
        name="tap_sums",
    )(padded, back_conv)


def backward_kernel(
    slot_ref, present_ref, slopes_ref, kernel_ref,
    centre_ref, outgoing_ref, piece_ref, border_ref, back_ref,
):
    channels = slopes_ref.shape[3]
    outgoing_ref[...] = jnp.zeros(outgoing_ref.shape, outgoing_ref.dtype)
    border_ref[...] = jnp.zeros(border_ref.shape, jnp.float32)
    for tile in range(slopes_ref.shape[0]):
        for tap_col in range(7):
            border_ref[tap_col, 6:22, tap_col : tap_col + 16, :] = slopes_ref[tile]
        for half in range(channels // LANES):
            lanes = pl.ds(half * LANES, LANES)

            def rows_back(step, carry):
                top = step * 2
                sums = [jnp.zeros((24, LANES), jnp.float32)] * 2
                for tap_col in range(7):
                    window = [border_ref[tap_col, top + row, :, lanes] for row in range(8)]
                    for tap_row in range(7):
                        weight = kernel_ref[pl.ds(7 * tap_row + tap_col, 1), lanes]
                        sums = [sums[row] + window[row + 6 - tap_row] * weight for row in range(2)]
                for row in range(2):
                    back_ref[top + row, :, lanes] = sums[row]
                return carry

            lax.fori_loop(0, 11, rows_back, 0)

        centre_ref[tile] = back_ref[3:19, 3:19, :]

        def send(direction):
            row = 8 * tile + direction
            strip = jnp.where(present_ref[row] > 0, piece_ref[...], 0.0)
            outgoing_ref[slot_ref[row]] = strip.astype(outgoing_ref.dtype)

        piece_ref[...] = back_ref[0:3, 3:19, :]
        send(0)
        piece_ref[...] = back_ref[19:22, 3:19, :]
        send(1)
        for direction, first in ((2, 0), (3, 19)):
            for depth in range(3):
                for place in range(16):
                    piece_ref[depth, pl.ds(place, 1)] = back_ref[
                        3 + place, pl.ds(first + depth, 1)
                    ]
            send(direction)
        for direction, top, left, taken in ((4, 0, 0, 13), (5, 0, 19, 0), (6, 19, 0, 13), (7, 19, 19, 0)):
            piece_ref[...] = jnp.zeros(piece_ref.shape, jnp.float32)
            piece_ref[:, taken : taken + 3, :] = back_ref[top : top + 3, left : left + 3, :]
            send(direction)


def backward_conv(back_conv, slot_index, present, kernel, slots):
    _, extent, _, channels = back_conv.shape
    return pl.pallas_call(
        backward_kernel,
        out_shape=(
            jax.ShapeDtypeStruct(back_conv.shape, jnp.float32),
            jax.ShapeDtypeStruct((slots, 3, extent, channels), jnp.bfloat16),
        ),
        in_specs=[SMEM, SMEM, VMEM, VMEM],
        out_specs=(VMEM, VMEM),
        scratch_shapes=[
            pltpu.VMEM((3, extent, channels), jnp.float32),
            pltpu.VMEM((7, extent + 12, extent + 8, channels), jnp.float32),
            pltpu.VMEM((extent + 6, extent + 8, channels), jnp.float32),
        ],
        compiler_params=pltpu.CompilerParams(vmem_limit_bytes=32 * 1024 * 1024),
        cost_estimate=estimate(7),
        name="backward_conv",
    )(slot_index, present, back_conv, kernel)


def collect_kernel(wanted_ref, base_ref, centre_ref, returned_ref, out_ref, table_ref):
    table_ref[...] = jnp.zeros(table_ref.shape, jnp.float32)

    def one(slot, carry):
        code = wanted_ref[slot]
        strip = returned_ref[slot].astype(jnp.float32)
        table_ref[jnp.maximum(code, 0)] += jnp.where(code >= 0, strip, 0.0)
        return carry

    lax.fori_loop(0, returned_ref.shape[0], one, 0)
    for tile in range(base_ref.shape[0]):
        out_ref[tile] = base_ref[tile].astype(jnp.float32) + centre_ref[tile]
        out_ref[tile, 0:3] += table_ref[4 * tile]
        out_ref[tile, 13:16] += table_ref[4 * tile + 1]
        for depth in range(3):
            for place in range(16):
                row = pl.ds(place, 1)
                out_ref[tile, place, pl.ds(depth, 1)] += table_ref[4 * tile + 2, depth, row]
                out_ref[tile, place, pl.ds(13 + depth, 1)] += table_ref[4 * tile + 3, depth, row]


def collect(base, centre, returned, wanted):
    tiles, extent, _, channels = base.shape
    return pl.pallas_call(
        collect_kernel,
        out_shape=jax.ShapeDtypeStruct(base.shape, jnp.float32),
        in_specs=[SMEM, VMEM, VMEM, VMEM],
        out_specs=VMEM,
        scratch_shapes=[pltpu.VMEM((4 * tiles, 3, extent, channels), jnp.float32)],
        compiler_params=pltpu.CompilerParams(vmem_limit_bytes=32 * 1024 * 1024),
        name="collect",
    )(wanted, base, centre, returned)


def normalize(conv, gain):
    average = jnp.mean(conv, axis=-1, keepdims=True)
    centred = conv - average
    spread = jnp.mean(centred * centred, axis=-1, keepdims=True)
    inverse = lax.rsqrt(spread + NORM_EPSILON)
    unit = centred * inverse
    return (unit, inverse, (unit * gain).astype(jnp.bfloat16))


def build_routes(source_device, source_slot, peers, capacity):
    row_total = source_slot.shape[0] * source_slot.shape[1]
    owner = source_device.reshape(row_total)
    codes = (source_slot * 4 + jnp.asarray(STRIP_KINDS, jnp.int32)[None, :]).reshape(row_total)
    later_rows = lax.broadcasted_iota(jnp.int32, (row_total, row_total), 0)
    other_rows = lax.broadcasted_iota(jnp.int32, (row_total, row_total), 1)
    before = jnp.logical_and(owner[:, None] == owner[None, :], other_rows < later_rows)
    ranking = jnp.sum(before.astype(jnp.int32), axis=1)
    slot_index = owner * capacity + ranking
    places = lax.broadcasted_iota(jnp.int32, (peers * capacity, row_total), 0)
    matched = (places == slot_index[None, :]).astype(jnp.int32)
    request = jnp.sum(matched * (codes[None, :] + 1), axis=1) - 1
    return (slot_index, request.reshape(peers, capacity))


def pair_term(operand_set):
    row_block, slope, rounded, hidden = operand_set
    dims_rows = (((0,), (0,)), ((), ()))
    first_term = lax.dot_general(row_block, slope, dims_rows, preferred_element_type=jnp.float32)
    second_term = lax.dot_general(rounded, hidden, dims_rows, preferred_element_type=jnp.float32)
    return jnp.stack([first_term, second_term], axis=1)


def halve(values, steps):
    index = lax.axis_index("tile")
    peers = 1 << steps
    values = values.reshape((peers, -1) + values.shape[1:])
    for step in range(steps):
        pairs = values.reshape((-1, 2) + values.shape[1:])
        bit = (index >> step) & 1
        kept = jnp.where(bit == 1, pairs[:, 1], pairs[:, 0])
        sent = jnp.where(bit == 1, pairs[:, 0], pairs[:, 1]).astype(jnp.bfloat16)
        partners = [(place, place ^ (1 << step)) for place in range(peers)]
        values = kept + lax.ppermute(sent, "tile", partners).astype(jnp.float32)
    return values[0]


def double(values, steps):
    peers = 1 << steps
    for step in range(steps):
        partners = [(place, place ^ (1 << step)) for place in range(peers)]
        values = values + lax.ppermute(values, "tile", partners)
    return values


def exchange(blocks, peers):
    arranged = blocks.reshape((peers, -1) + blocks.shape[1:])
    returned = lax.all_to_all(arranged, "tile", split_axis=0, concat_axis=0, tiled=True)
    return returned.reshape(blocks.shape)


def body(
    tiles, source_device, source_slot, present, depth_kernel, norm_gain, w_in, w_out, cotangent
):
    peers = lax.axis_size("tile")
    local_tiles = tiles.shape[0]
    extent = tiles.shape[1]
    channels = tiles.shape[3]
    layers = w_in.shape[0]
    capacity = max(2, 2 * ((8 * local_tiles + peers - 1) // peers))
    scale = 1.0 / math.sqrt(local_tiles * peers * extent * extent)
    slot_index, request = build_routes(source_device, source_slot, peers, capacity)
    framed = jnp.pad(request[:, None, :], ((0, 0), (0, 7), (0, 128 - capacity)))
    wanted = direct_exchange(framed.reshape(peers * 8, 128), peers, 0)
    wanted = wanted.reshape(peers, 8, 128)[:, 0, :capacity].reshape(-1)
    present = present.reshape(-1)
    dims_cols = (((1,), (1,)), ((), ()))
    saved = []
    current = tiles
    for layer_index in range(layers):
        incoming = direct_exchange(serve(current, wanted), peers, 1)
        padded, conv = forward_conv(
            current, incoming, slot_index, present, depth_kernel[layer_index]
        )
        unit, inverse, normed = normalize(conv, norm_gain[layer_index])
        row_block = normed.reshape(-1, channels)
        pre = jnp.dot(row_block, w_in[layer_index], preferred_element_type=jnp.float32)
        hidden = gelu_value(pre).astype(jnp.bfloat16)
        mixed = jnp.dot(hidden, w_out[layer_index], preferred_element_type=jnp.float32)
        kept = padded
        saved.append(
            (
                current,
                kept,
                unit.reshape(-1, channels),
                inverse.reshape(-1, 1),
                row_block,
                pre,
                hidden,
            )
        )
        current = (current.astype(jnp.float32) + mixed.reshape(current.shape)).astype(jnp.bfloat16)
    gradient = cotangent.astype(jnp.float32)
    weight_terms = [None] * layers
    small_terms = [None] * layers
    steps = peers.bit_length() - 1
    for layer_index in reversed(range(layers)):
        inputs, kept, unit, inverse, row_block, pre, hidden = saved[layer_index]
        rounded = gradient.astype(jnp.bfloat16).reshape(-1, channels)
        back_hidden = lax.dot_general(
            rounded, w_out[layer_index], dims_cols, preferred_element_type=jnp.float32
        )
        slope = (back_hidden * gelu_slope(pre)).astype(jnp.bfloat16)
        back_norm = lax.dot_general(
            slope, w_in[layer_index], dims_cols, preferred_element_type=jnp.float32
        )
        operand_set = (row_block, slope, rounded, hidden)
        scaled_back = back_norm * norm_gain[layer_index]
        gain_term = jnp.sum(back_norm * unit, axis=0)
        first_mean = jnp.mean(scaled_back, axis=-1, keepdims=True)
        second_mean = jnp.mean(scaled_back * unit, axis=-1, keepdims=True)
        back_conv = (inverse * (scaled_back - first_mean - unit * second_mean)).reshape(
            inputs.shape
        )
        centre, outgoing = backward_conv(
            back_conv, slot_index, present, depth_kernel[layer_index], peers * capacity
        )
        if layer_index > 0:
            outgoing, back_conv, slope = lax.optimization_barrier((outgoing, back_conv, slope))
            operand_set = (row_block, slope, rounded, hidden)
        weight_terms[layer_index] = halve(pair_term(operand_set), steps)
        kernel_term = tap_sums(kept, back_conv)
        small_terms[layer_index] = double(
            jnp.concatenate([kernel_term, gain_term[None]], axis=0), steps
        )
        gradient = collect(gradient, centre, exchange(outgoing, peers), wanted)
    weights_part = jnp.stack(weight_terms, axis=2)
    small = jnp.stack(small_terms)
    kernel_sum, gain_sum = small[:, :-1], small[:, -1]
    grad_tiles = gradient.astype(jnp.bfloat16)
    return (
        grad_tiles,
        weights_part[:, 0] * scale,
        weights_part[:, 1] * scale,
        kernel_sum * scale,
        gain_sum * scale,
    )


def solution(mesh):
    return jax.shard_map(
        body,
        mesh=mesh,
        in_specs=(
            P(("parts", "tile"), None, None, None),
            P(("parts", "tile"), None, None),
            P(("parts", "tile"), None),
            P(("parts", "tile"), None),
            P(),
            P(),
            P(),
            P(),
            P(("parts", "tile"), None, None, None),
        ),
        out_specs=(
            P(("parts", "tile"), None, None, None),
            P(("parts", "tile"), None, None),
            P(("parts", "tile"), None, None),
            P("parts", None, None),
            P("parts", None),
        ),
        check_vma=False,
    )
```

```python
import functools
import math

import jax
import jax.numpy as jnp
from jax import lax
from jax.experimental import pallas as pl
from jax.experimental.pallas import tpu as pltpu
from jax.sharding import PartitionSpec as P

STRIP_KINDS = (1, 0, 3, 2, 1, 1, 0, 0)
NORM_EPSILON = 1e-06
ROOT_HALF = 0.7071067811865476
INV_ROOT_TWO_PI = 0.3989422804014327


def gelu_value(values):
    return values * 0.5 * (1.0 + lax.erf(values * ROOT_HALF))


def gelu_slope(values):
    return 0.5 * (1.0 + lax.erf(values * ROOT_HALF)) + values * INV_ROOT_TWO_PI * jnp.exp(
        -0.5 * values * values
    )


LANES = 128
SMEM = pl.BlockSpec(memory_space=pltpu.SMEM)
VMEM = pl.BlockSpec(memory_space=pltpu.VMEM)


def estimate(microseconds):
    return pl.CostEstimate(
        flops=int(microseconds * 1.1e9), bytes_accessed=int(microseconds * 3.6e6), transcendentals=0
    )


def exchange_kernel(peers, source_ref, target_ref, send_sem, recv_sem, own_sem):
    me = lax.axis_index("tile")
    barrier = pltpu.get_barrier_semaphore()

    def greet(offset, carry):
        pl.semaphore_signal(
            barrier,
            inc=1,
            device_id={"tile": lax.rem(me + offset, peers)},
            device_id_type=pl.DeviceIdType.MESH,
        )
        return carry

    def remote(offset):
        other = lax.rem(me + offset, peers)
        return pltpu.make_async_remote_copy(
            src_ref=source_ref.at[other],
            dst_ref=target_ref.at[me],
            send_sem=send_sem.at[offset],
            recv_sem=recv_sem.at[offset],
            device_id={"tile": other},
            device_id_type=pl.DeviceIdType.MESH,
        )

    def begin(offset, carry):
        remote(offset).start()
        return carry

    def finish(offset, carry):
        remote(offset).wait()
        return carry

    lax.fori_loop(1, peers, greet, 0)
    pl.semaphore_wait(barrier, peers - 1)
    lax.fori_loop(1, peers, begin, 0)
    own = pltpu.make_async_copy(source_ref.at[me], target_ref.at[me], own_sem)
    own.start()
    lax.fori_loop(1, peers, finish, 0)
    own.wait()


def direct_exchange(blocks, peers, identity):
    arranged = blocks.reshape((peers, -1) + blocks.shape[1:])
    returned = pl.pallas_call(
        functools.partial(exchange_kernel, peers),
        out_shape=jax.ShapeDtypeStruct(arranged.shape, arranged.dtype),
        in_specs=[VMEM],
        out_specs=VMEM,
        scratch_shapes=[
            pltpu.SemaphoreType.DMA((peers,)),
            pltpu.SemaphoreType.DMA((peers,)),
            pltpu.SemaphoreType.DMA,
        ],
        compiler_params=pltpu.CompilerParams(
            collective_id=identity, has_side_effects=True, vmem_limit_bytes=16 * 1024 * 1024
        ),
        name="exchange_requests" if identity == 0 else "exchange_strips",
    )(arranged)
    return returned.reshape(blocks.shape)


def serve_kernel(wanted_ref, inputs_ref, out_ref, wide_ref, table_ref):
    for tile in range(inputs_ref.shape[0]):
        wide_ref[...] = inputs_ref[tile].astype(jnp.float32)
        table_ref[4 * tile] = wide_ref[0:3]
        table_ref[4 * tile + 1] = wide_ref[13:16]
        for depth in range(3):
            for place in range(16):
                row = pl.ds(place, 1)
                table_ref[4 * tile + 2, depth, row] = wide_ref[place, pl.ds(depth, 1)]
                table_ref[4 * tile + 3, depth, row] = wide_ref[place, pl.ds(13 + depth, 1)]

    def one(slot, carry):
        code = wanted_ref[slot]
        strip = table_ref[jnp.maximum(code, 0)]
        out_ref[slot] = jnp.where(code >= 0, strip, 0.0).astype(out_ref.dtype)
        return carry

    lax.fori_loop(0, out_ref.shape[0], one, 0)


def serve(inputs, wanted):
    tiles, extent, _, channels = inputs.shape
    return pl.pallas_call(
        serve_kernel,
        out_shape=jax.ShapeDtypeStruct((wanted.shape[0], 3, extent, channels), jnp.bfloat16),
        in_specs=[SMEM, VMEM],
        out_specs=VMEM,
        scratch_shapes=[
            pltpu.VMEM((extent, extent, channels), jnp.float32),
            pltpu.VMEM((4 * tiles, 3, extent, channels), jnp.float32),
        ],
        compiler_params=pltpu.CompilerParams(vmem_limit_bytes=32 * 1024 * 1024),
        name="serve",
    )(wanted, inputs)


def shift_columns(padded_ref, tile, shifted_ref):
    for tap_col in range(7):
        shifted_ref[tap_col] = padded_ref[tile, :, tap_col : tap_col + 16, :]


def forward_kernel(
    slot_ref, present_ref, inputs_ref, incoming_ref, kernel_ref, padded_ref, conv_ref, piece_ref, shifted_ref
):
    for tile in range(inputs_ref.shape[0]):

        def piece(direction):
            row = 8 * tile + direction
            strip = incoming_ref[slot_ref[row]].astype(jnp.float32)
            return jnp.where(present_ref[row] > 0, strip, 0.0)

        padded_ref[tile, 3:19, 3:19, :] = inputs_ref[tile].astype(jnp.float32)
        padded_ref[tile, 0:3, 3:19, :] = piece(0)
        padded_ref[tile, 19:22, 3:19, :] = piece(1)
        for direction, first in ((2, 0), (3, 19)):
            piece_ref[...] = piece(direction)
            for depth in range(3):
                for place in range(16):
                    padded_ref[tile, 3 + place, pl.ds(first + depth, 1)] = piece_ref[
                        depth, pl.ds(place, 1)
                    ]
        for direction, top, left, taken in ((4, 0, 0, 13), (5, 0, 19, 0), (6, 19, 0, 13), (7, 19, 19, 0)):
            piece_ref[...] = piece(direction)
            padded_ref[tile, top : top + 3, left : left + 3, :] = piece_ref[:, taken : taken + 3, :]
        padded_ref[tile, :, 22:24, :] = jnp.zeros((22, 2, padded_ref.shape[3]), jnp.float32)
        shift_columns(padded_ref, tile, shifted_ref)
        for half in range(conv_ref.shape[3] // LANES):
            lanes = pl.ds(half * LANES, LANES)

            def rows(step, carry):
                top = step * 4
                sums = [jnp.zeros((16, LANES), jnp.float32)] * 4
                for tap_col in range(7):
                    window = [shifted_ref[tap_col, top + row, :, lanes] for row in range(10)]
                    for tap_row in range(7):
                        weight = kernel_ref[pl.ds(7 * tap_row + tap_col, 1), lanes]
                        sums = [sums[row] + window[row + tap_row] * weight for row in range(4)]
                for row in range(4):
                    conv_ref[tile, top + row, :, lanes] = sums[row]
                return carry

            lax.fori_loop(0, 4, rows, 0)


def forward_conv(inputs, incoming, slot_index, present, kernel):
    tiles, extent, _, channels = inputs.shape
    return pl.pallas_call(
        forward_kernel,
        out_shape=(
            jax.ShapeDtypeStruct((tiles, extent + 6, extent + 8, channels), jnp.float32),
            jax.ShapeDtypeStruct((tiles, extent, extent, channels), jnp.float32),
        ),
        in_specs=[SMEM, SMEM, VMEM, VMEM, VMEM],
        out_specs=(VMEM, VMEM),
        scratch_shapes=[
            pltpu.VMEM((3, extent, channels), jnp.float32),
            pltpu.VMEM((7, extent + 6, extent, channels), jnp.float32),
        ],
        compiler_params=pltpu.CompilerParams(vmem_limit_bytes=32 * 1024 * 1024),
        name="forward_conv",
    )(slot_index, present, inputs, incoming, kernel)


def taps_kernel(padded_ref, slopes_ref, taps_ref, shifted_ref, sums_ref):
    channels = slopes_ref.shape[3]
    for tile in range(slopes_ref.shape[0]):
        shift_columns(padded_ref, tile, shifted_ref)
        for half in range(channels // LANES):
            lanes = pl.ds(half * LANES, LANES)

            def taps(tap_col, carry):
                def rows(step, sums):
                    top = step * 4
                    slopes = [slopes_ref[tile, top + row, :, lanes] for row in range(4)]
                    window = [shifted_ref[tap_col, top + row, :, lanes] for row in range(10)]
                    return tuple(
                        sums[tap_row]
                        + (
                            window[tap_row] * slopes[0]
                            + window[tap_row + 1] * slopes[1]
                            + window[tap_row + 2] * slopes[2]
                            + window[tap_row + 3] * slopes[3]
                        )
                        for tap_row in range(7)
                    )

                sums = lax.fori_loop(0, 4, rows, (jnp.zeros((16, LANES), jnp.float32),) * 7)
                for tap_row in range(7):
                    if tile == 0:
                        sums_ref[tap_col, tap_row, :, lanes] = sums[tap_row]
                    else:
                        sums_ref[tap_col, tap_row, :, lanes] += sums[tap_row]
                return carry

            lax.fori_loop(0, 7, taps, 0)
    for tap_col in range(7):
        for tap_row in range(7):
            taps_ref[pl.ds(7 * tap_row + tap_col, 1)] = jnp.sum(
                sums_ref[tap_col, tap_row], axis=0, keepdims=True
            )


def tap_sums(padded, back_conv):
    _, extent, _, channels = back_conv.shape
    return pl.pallas_call(
        taps_kernel,
        out_shape=jax.ShapeDtypeStruct((49, channels), jnp.float32),
        in_specs=[VMEM, VMEM],
        out_specs=VMEM,
        scratch_shapes=[
            pltpu.VMEM((7, extent + 6, extent, channels), jnp.float32),
            pltpu.VMEM((7, 7, extent, channels), jnp.float32),
        ],
        compiler_params=pltpu.CompilerParams(vmem_limit_bytes=32 * 1024 * 1024),
        cost_estimate=estimate(5),
        name="tap_sums",
    )(padded, back_conv)


def backward_kernel(
    slot_ref, present_ref, slopes_ref, kernel_ref,
    centre_ref, outgoing_ref, piece_ref, border_ref, back_ref,
):
    channels = slopes_ref.shape[3]
    outgoing_ref[...] = jnp.zeros(outgoing_ref.shape, outgoing_ref.dtype)
    border_ref[...] = jnp.zeros(border_ref.shape, jnp.float32)
    for tile in range(slopes_ref.shape[0]):
        for tap_col in range(7):
            border_ref[tap_col, 6:22, tap_col : tap_col + 16, :] = slopes_ref[tile]
        for half in range(channels // LANES):
            lanes = pl.ds(half * LANES, LANES)

            def rows_back(step, carry):
                top = step * 2
                sums = [jnp.zeros((24, LANES), jnp.float32)] * 2
                for tap_col in range(7):
                    window = [border_ref[tap_col, top + row, :, lanes] for row in range(8)]
                    for tap_row in range(7):
                        weight = kernel_ref[pl.ds(7 * tap_row + tap_col, 1), lanes]
                        sums = [sums[row] + window[row + 6 - tap_row] * weight for row in range(2)]
                for row in range(2):
                    back_ref[top + row, :, lanes] = sums[row]
                return carry

            lax.fori_loop(0, 11, rows_back, 0)

        centre_ref[tile] = back_ref[3:19, 3:19, :]

        def send(direction):
            row = 8 * tile + direction
            strip = jnp.where(present_ref[row] > 0, piece_ref[...], 0.0)
            outgoing_ref[slot_ref[row]] = strip.astype(outgoing_ref.dtype)

        piece_ref[...] = back_ref[0:3, 3:19, :]
        send(0)
        piece_ref[...] = back_ref[19:22, 3:19, :]
        send(1)
        for direction, first in ((2, 0), (3, 19)):
            for depth in range(3):
                for place in range(16):
                    piece_ref[depth, pl.ds(place, 1)] = back_ref[
                        3 + place, pl.ds(first + depth, 1)
                    ]
            send(direction)
        for direction, top, left, taken in ((4, 0, 0, 13), (5, 0, 19, 0), (6, 19, 0, 13), (7, 19, 19, 0)):
            piece_ref[...] = jnp.zeros(piece_ref.shape, jnp.float32)
            piece_ref[:, taken : taken + 3, :] = back_ref[top : top + 3, left : left + 3, :]
            send(direction)


def backward_conv(back_conv, slot_index, present, kernel, slots):
    _, extent, _, channels = back_conv.shape
    return pl.pallas_call(
        backward_kernel,
        out_shape=(
            jax.ShapeDtypeStruct(back_conv.shape, jnp.float32),
            jax.ShapeDtypeStruct((slots, 3, extent, channels), jnp.bfloat16),
        ),
        in_specs=[SMEM, SMEM, VMEM, VMEM],
        out_specs=(VMEM, VMEM),
        scratch_shapes=[
            pltpu.VMEM((3, extent, channels), jnp.float32),
            pltpu.VMEM((7, extent + 12, extent + 8, channels), jnp.float32),
            pltpu.VMEM((extent + 6, extent + 8, channels), jnp.float32),
        ],
        compiler_params=pltpu.CompilerParams(vmem_limit_bytes=32 * 1024 * 1024),
        cost_estimate=estimate(7),
        name="backward_conv",
    )(slot_index, present, back_conv, kernel)


def collect_kernel(wanted_ref, base_ref, centre_ref, returned_ref, out_ref, table_ref):
    table_ref[...] = jnp.zeros(table_ref.shape, jnp.float32)

    def one(slot, carry):
        code = wanted_ref[slot]
        strip = returned_ref[slot].astype(jnp.float32)
        table_ref[jnp.maximum(code, 0)] += jnp.where(code >= 0, strip, 0.0)
        return carry

    lax.fori_loop(0, returned_ref.shape[0], one, 0)
    for tile in range(base_ref.shape[0]):
        out_ref[tile] = base_ref[tile].astype(jnp.float32) + centre_ref[tile]
        out_ref[tile, 0:3] += table_ref[4 * tile]
        out_ref[tile, 13:16] += table_ref[4 * tile + 1]
        for depth in range(3):
            for place in range(16):
                row = pl.ds(place, 1)
                out_ref[tile, place, pl.ds(depth, 1)] += table_ref[4 * tile + 2, depth, row]
                out_ref[tile, place, pl.ds(13 + depth, 1)] += table_ref[4 * tile + 3, depth, row]


def collect(base, centre, returned, wanted):
    tiles, extent, _, channels = base.shape
    return pl.pallas_call(
        collect_kernel,
        out_shape=jax.ShapeDtypeStruct(base.shape, jnp.float32),
        in_specs=[SMEM, VMEM, VMEM, VMEM],
        out_specs=VMEM,
        scratch_shapes=[pltpu.VMEM((4 * tiles, 3, extent, channels), jnp.float32)],
        compiler_params=pltpu.CompilerParams(vmem_limit_bytes=32 * 1024 * 1024),
        name="collect",
    )(wanted, base, centre, returned)


def normalize(conv, gain):
    average = jnp.mean(conv, axis=-1, keepdims=True)
    centred = conv - average
    spread = jnp.mean(centred * centred, axis=-1, keepdims=True)
    inverse = lax.rsqrt(spread + NORM_EPSILON)
    unit = centred * inverse
    return (unit, inverse, (unit * gain).astype(jnp.bfloat16))


def build_routes(source_device, source_slot, peers, capacity):
    row_total = source_slot.shape[0] * source_slot.shape[1]
    owner = source_device.reshape(row_total)
    codes = (source_slot * 4 + jnp.asarray(STRIP_KINDS, jnp.int32)[None, :]).reshape(row_total)
    later_rows = lax.broadcasted_iota(jnp.int32, (row_total, row_total), 0)
    other_rows = lax.broadcasted_iota(jnp.int32, (row_total, row_total), 1)
    before = jnp.logical_and(owner[:, None] == owner[None, :], other_rows < later_rows)
    ranking = jnp.sum(before.astype(jnp.int32), axis=1)
    slot_index = owner * capacity + ranking
    places = lax.broadcasted_iota(jnp.int32, (peers * capacity, row_total), 0)
    matched = (places == slot_index[None, :]).astype(jnp.int32)
    request = jnp.sum(matched * (codes[None, :] + 1), axis=1) - 1
    return (slot_index, request.reshape(peers, capacity))


def pair_term(operand_set):
    row_block, slope, rounded, hidden = operand_set
    dims_rows = (((0,), (0,)), ((), ()))
    first_term = lax.dot_general(row_block, slope, dims_rows, preferred_element_type=jnp.float32)
    second_term = lax.dot_general(rounded, hidden, dims_rows, preferred_element_type=jnp.float32)
    return jnp.stack([first_term, second_term], axis=1)


def halve(values, steps):
    index = lax.axis_index("tile")
    peers = 1 << steps
    values = values.reshape((peers, -1) + values.shape[1:])
    for step in range(steps):
        pairs = values.reshape((-1, 2) + values.shape[1:])
        bit = (index >> step) & 1
        kept = jnp.where(bit == 1, pairs[:, 1], pairs[:, 0])
        sent = jnp.where(bit == 1, pairs[:, 0], pairs[:, 1]).astype(jnp.bfloat16)
        partners = [(place, place ^ (1 << step)) for place in range(peers)]
        values = kept + lax.ppermute(sent, "tile", partners).astype(jnp.float32)
    return values[0]


def double(values, steps):
    peers = 1 << steps
    for step in range(steps):
        partners = [(place, place ^ (1 << step)) for place in range(peers)]
        values = values + lax.ppermute(values, "tile", partners)
    return values


def exchange(blocks, peers):
    arranged = blocks.reshape((peers, -1) + blocks.shape[1:])
    returned = lax.all_to_all(arranged, "tile", split_axis=0, concat_axis=0, tiled=True)
    return returned.reshape(blocks.shape)


def body(
    tiles, source_device, source_slot, present, depth_kernel, norm_gain, w_in, w_out, cotangent
):
    peers = lax.axis_size("tile")
    local_tiles = tiles.shape[0]
    extent = tiles.shape[1]
    channels = tiles.shape[3]
    layers = w_in.shape[0]
    capacity = max(2, 2 * ((8 * local_tiles + peers - 1) // peers))
    scale = 1.0 / math.sqrt(local_tiles * peers * extent * extent)
    slot_index, request = build_routes(source_device, source_slot, peers, capacity)
    framed = jnp.pad(request[:, None, :], ((0, 0), (0, 7), (0, 128 - capacity)))
    wanted = direct_exchange(framed.reshape(peers * 8, 128), peers, 0)
    wanted = wanted.reshape(peers, 8, 128)[:, 0, :capacity].reshape(-1)
    present = present.reshape(-1)
    dims_cols = (((1,), (1,)), ((), ()))
    saved = []
    current = tiles
    for layer_index in range(layers):
        incoming = direct_exchange(serve(current, wanted), peers, 1)
        padded, conv = forward_conv(
            current, incoming, slot_index, present, depth_kernel[layer_index]
        )
        unit, inverse, normed = normalize(conv, norm_gain[layer_index])
        row_block = normed.reshape(-1, channels)
        pre = jnp.dot(row_block, w_in[layer_index], preferred_element_type=jnp.float32)
        hidden = gelu_value(pre).astype(jnp.bfloat16)
        mixed = jnp.dot(hidden, w_out[layer_index], preferred_element_type=jnp.float32)
        kept = padded
        saved.append(
            (
                current,
                kept,
                unit.reshape(-1, channels),
                inverse.reshape(-1, 1),
                row_block,
                pre,
                hidden,
            )
        )
        current = (current.astype(jnp.float32) + mixed.reshape(current.shape)).astype(jnp.bfloat16)
    gradient = cotangent.astype(jnp.float32)
    weight_terms = [None] * layers
    small_terms = [None] * layers
    steps = peers.bit_length() - 1
    for layer_index in reversed(range(layers)):
        inputs, kept, unit, inverse, row_block, pre, hidden = saved[layer_index]
        rounded = gradient.astype(jnp.bfloat16).reshape(-1, channels)
        back_hidden = lax.dot_general(
            rounded, w_out[layer_index], dims_cols, preferred_element_type=jnp.float32
        )
        slope = (back_hidden * gelu_slope(pre)).astype(jnp.bfloat16)
        back_norm = lax.dot_general(
            slope, w_in[layer_index], dims_cols, preferred_element_type=jnp.float32
        )
        operand_set = (row_block, slope, rounded, hidden)
        scaled_back = back_norm * norm_gain[layer_index]
        gain_term = jnp.sum(back_norm * unit, axis=0)
        first_mean = jnp.mean(scaled_back, axis=-1, keepdims=True)
        second_mean = jnp.mean(scaled_back * unit, axis=-1, keepdims=True)
        back_conv = (inverse * (scaled_back - first_mean - unit * second_mean)).reshape(
            inputs.shape
        )
        centre, outgoing = backward_conv(
            back_conv, slot_index, present, depth_kernel[layer_index], peers * capacity
        )
        if layer_index > 0:
            outgoing, back_conv, slope = lax.optimization_barrier((outgoing, back_conv, slope))
            operand_set = (row_block, slope, rounded, hidden)
        terms = pair_term(operand_set)
        small_terms[layer_index] = jnp.concatenate(
            [tap_sums(kept, back_conv), gain_term[None]], axis=0
        )
        if layer_index > 0:
            returned = exchange(outgoing, peers)
            returned, terms = lax.optimization_barrier((returned, terms))
        else:
            returned = direct_exchange(outgoing, peers, 1)
        weight_terms[layer_index] = halve(terms, steps)
        gradient = collect(gradient, centre, returned, wanted)
    weights_part = jnp.stack(weight_terms, axis=2)
    small = double(jnp.stack(small_terms), steps)
    kernel_sum, gain_sum = small[:, :-1], small[:, -1]
    grad_tiles = gradient.astype(jnp.bfloat16)
    return (
        grad_tiles,
        weights_part[:, 0] * scale,
        weights_part[:, 1] * scale,
        kernel_sum * scale,
        gain_sum * scale,
    )


def solution(mesh):
    return jax.shard_map(
        body,
        mesh=mesh,
        in_specs=(
            P(("parts", "tile"), None, None, None),
            P(("parts", "tile"), None, None),
            P(("parts", "tile"), None),
            P(("parts", "tile"), None),
            P(),
            P(),
            P(),
            P(),
            P(("parts", "tile"), None, None, None),
        ),
        out_specs=(
            P(("parts", "tile"), None, None, None),
            P(("parts", "tile"), None, None),
            P(("parts", "tile"), None, None),
            P("parts", None, None),
            P("parts", None),
        ),
        check_vma=False,
    )
```
